32 devices in a mesh: ctx: 8 (over z, x), ts: 4 (over y, core).
Axes of the slice: x: 2, y: 2, z: 4, core: 2. Of those that a mesh axis runs over, the one named last changes fastest.
Arguments:
- se_input: bfloat16 [2048, 3, 4096], P('ctx', None, 'ts'), may hold values from -6 to 6
- mr_input: bfloat16 [2048, 2, 4096], P('ctx', None, 'ts'), may hold values from -6 to 6
- cotangent: bfloat16 [2048, 4096], P('ctx', 'ts'), may hold values from -6 to 6
- se_featurizer: float32 [3, 3, 4096], P(None, None, 'ts'), may hold values from -3.5 to 3.5
- mr_featurizer: float32 [3, 3, 4096], P(None, None, 'ts'), may hold values from -3.5 to 3.5
- se_filter: float32 [7, 4096], P(None, 'ts'), may hold values from -2 to 2
- mr_filter: float32 [128, 4096], P(None, 'ts'), may hold values from -1 to 1
- decay_rate: float32 [4096], P('ts'), may hold values from 0.003 to 0.05
Outputs:
- grad_se_input: bfloat16 [2048, 3, 4096], P('ctx', None, 'ts')
- grad_mr_input: bfloat16 [2048, 2, 4096], P('ctx', None, 'ts')
- grad_se_filter: float32 [7, 4096], P(None, 'ts')
- grad_mr_filter: float32 [128, 4096], P(None, 'ts')
The draws below stay inside these ranges and needn't reach their ends.
All inputs are finite; a program needn't handle non-finite values.
Results may differ from the reference program's by a relative error of at most 0.0061.
Values may be sent and summed in bfloat16 or wider, within the bound.
A program may use at most 128 MiB of HBM per device.

```python
import math
import jax
import jax.numpy as jnp
from jax import lax

C = 4096
LF = 3
LS = 7
LM = 128
TOKENS = 2048


def block_levels(stream_key, extent, split, smallest, largest):
    def one(axis_at, blocks):
        steps = jax.random.uniform(jax.random.fold_in(jax.random.fold_in(stream_key, 6), axis_at), (blocks,), jnp.float32, smallest / len(split), largest / len(split))
        return jnp.repeat(jnp.exp(steps), extent[axis_at] // blocks).reshape((-1,) + (1,) * (len(extent) - axis_at - 1))

    gain = one(*split[0])
    for cut in split[1:]:
        gain = gain * one(*cut)
    return gain


def bell_draw(rng, dims, deviation, limit, cuts=(), kind=jnp.bfloat16):
    factor_of = block_levels(rng, dims, cuts, -0.22, 0.18) if cuts else 1.0
    values = jax.random.normal(rng, dims, jnp.float32) * deviation * factor_of
    return jnp.minimum(jnp.maximum(values, -limit), limit).astype(kind)


def setup_inputs(seed: int = 0) -> dict:
    keys = jax.random.split(jax.random.key(seed), 9)
    return {
        "se_input": bell_draw(keys[0], (TOKENS, 3, C), 1.0, 6.0, ((0, 8), (2, 4))),
        "mr_input": bell_draw(keys[1], (TOKENS, 2, C), 1.0, 6.0, ((0, 8), (2, 4))),
        "cotangent": bell_draw(keys[2], (TOKENS, C), 1.0, 6.0, ((0, 8), (1, 4))),
        "se_featurizer": bell_draw(keys[3], (LF, 3, C), LF ** -0.5, 3.5, ((2, 4),), jnp.float32),
        "mr_featurizer": bell_draw(keys[4], (LF, 3, C), LF ** -0.5, 3.5, ((2, 4),), jnp.float32),
        "se_filter": bell_draw(keys[5], (LS, C), LS ** -0.5, 2.0, ((1, 4),), jnp.float32),
        "mr_filter": bell_draw(keys[6], (LM, C), (LM // 4) ** -0.5, 1.0, ((1, 4),), jnp.float32),
        "decay_rate": jnp.clip(jnp.exp(math.log(0.05) - 2.8134107 * jax.random.uniform(keys[7], (C,), jnp.float32) ** block_levels(keys[7], (C,), ((0, 4),), -0.2, 0.2)), 0.003, 0.05),
    }


def causal_sum(signal, kernel):
    tap_count = kernel.shape[0]
    row_count = signal.shape[0]
    padded = jnp.pad(signal, ((tap_count - 1, 0), (0, 0)))
    summed = jnp.zeros_like(signal)
    for offset in range(tap_count):
        begin = tap_count - 1 - offset
        summed = summed + kernel[offset] * padded[begin:begin + row_count]
    return summed

def ahead_sum(signal, kernel):
    tap_count = kernel.shape[0]
    row_count = signal.shape[0]
    padded = jnp.pad(signal, ((0, tap_count - 1), (0, 0)))
    summed = jnp.zeros_like(signal)
    for offset in range(tap_count):
        summed = summed + kernel[offset] * padded[offset:offset + row_count]
    return summed

def lag_sums(upstream, history, tap_count):
    row_count = upstream.shape[0]
    padded = jnp.pad(history, ((tap_count - 1, 0), (0, 0)))
    pieces = []
    for offset in range(tap_count):
        begin = tap_count - 1 - offset
        pieces.append(lax.optimization_barrier(jnp.sum(upstream * padded[begin:begin + row_count], axis=0)))
    return jnp.stack(pieces, axis=0)

def reference(se_input, mr_input, cotangent, se_featurizer, mr_featurizer, se_filter, mr_filter, decay_rate):
    block_width = min(128, C)
    block_count = C // block_width
    norm_factor = 1.0 / math.sqrt(TOKENS)
    lag_steps = jnp.arange(LM, dtype=jnp.float32)[:, None]

    def columns(source, start):
        return lax.dynamic_slice_in_dim(source, start, block_width, axis=1)

    def part_columns(source, part, start):
        return lax.dynamic_slice_in_dim(source[:, part, :], start, block_width, axis=1)

    def one_block(block_index):
        start = (block_index * block_width).astype(jnp.int32)
        se_query_taps = part_columns(se_featurizer, 0, start)
        se_key_taps = part_columns(se_featurizer, 1, start)
        se_value_taps = part_columns(se_featurizer, 2, start)
        mr_query_taps = part_columns(mr_featurizer, 0, start)
        mr_key_taps = part_columns(mr_featurizer, 1, start)
        mr_value_taps = part_columns(mr_featurizer, 2, start)
        query_one = causal_sum(part_columns(se_input, 0, start).astype(jnp.float32), se_query_taps)
        key_one = causal_sum(part_columns(se_input, 1, start).astype(jnp.float32), se_key_taps)
        value_one = causal_sum(part_columns(se_input, 2, start).astype(jnp.float32), se_value_taps)
        product_one = (key_one * value_one).astype(jnp.bfloat16).astype(jnp.float32)
        short_kernel = columns(se_filter, start)
        mixed_one = causal_sum(product_one, short_kernel)
        output_one = (query_one * mixed_one).astype(jnp.bfloat16)
        query_two = causal_sum(part_columns(mr_input, 0, start).astype(jnp.float32), mr_query_taps)
        key_two = causal_sum(part_columns(mr_input, 1, start).astype(jnp.float32), mr_key_taps)
        value_two = causal_sum(output_one.astype(jnp.float32), mr_value_taps)
        product_two = (key_two * value_two).astype(jnp.bfloat16).astype(jnp.float32)
        rates = lax.dynamic_slice_in_dim(decay_rate, start, block_width)
        damping = jnp.exp(-lag_steps * rates[None, :])
        medium_kernel = columns(mr_filter, start) * damping
        mixed_two = causal_sum(product_two, medium_kernel)
        upstream = columns(cotangent, start).astype(jnp.float32)
        grad_query_two = upstream * mixed_two
        grad_mixed_two = upstream * query_two
        grad_product_two = ahead_sum(grad_mixed_two, medium_kernel)
        medium_grad = lag_sums(grad_mixed_two, product_two, LM) * damping * norm_factor
        grad_mr_query = ahead_sum(grad_query_two, mr_query_taps)
        grad_mr_key = ahead_sum(grad_product_two * value_two, mr_key_taps)
        grad_output_one = ahead_sum(grad_product_two * key_two, mr_value_taps)
        grad_query_one = grad_output_one * mixed_one
        grad_mixed_one = grad_output_one * query_one
        grad_product_one = ahead_sum(grad_mixed_one, short_kernel)
        short_grad = lag_sums(grad_mixed_one, product_one, LS) * norm_factor
        grad_se_query = ahead_sum(grad_query_one, se_query_taps)
        grad_se_key = ahead_sum(grad_product_one * value_one, se_key_taps)
        grad_se_value = ahead_sum(grad_product_one * key_one, se_value_taps)
        se_parts = jnp.stack([grad_se_query, grad_se_key, grad_se_value], axis=0).astype(jnp.bfloat16)
        mr_parts = jnp.stack([grad_mr_query, grad_mr_key], axis=0).astype(jnp.bfloat16)
        return (se_parts, mr_parts, short_grad, medium_grad)
    se_parts, mr_parts, short_grads, medium_grads = lax.map(one_block, jnp.arange(block_count, dtype=jnp.int32))
    grad_se_input = jnp.transpose(se_parts, (2, 1, 0, 3)).reshape(TOKENS, 3, C)
    grad_mr_input = jnp.transpose(mr_parts, (2, 1, 0, 3)).reshape(TOKENS, 2, C)
    grad_se_filter = jnp.transpose(short_grads, (1, 0, 2)).reshape(LS, C)
    grad_mr_filter = jnp.transpose(medium_grads, (1, 0, 2)).reshape(LM, C)
    return (grad_se_input, grad_mr_input, grad_se_filter, grad_mr_filter)
```

```python
import functools
import math

import jax
import jax.numpy as jnp
import numpy as np
from jax import lax
from jax.experimental import pallas as pl
from jax.experimental.pallas import tpu as pltpu
from jax.sharding import PartitionSpec as P

F32 = jnp.float32
BF16 = jnp.bfloat16
EDGE = 16
PAD = 8


def round_up(value, unit):
    return -(-value // unit) * unit


def transforms(rows, taps):
    behind = taps
    span = behind + rows + EDGE
    n = round_up(span, 32)
    half = n // 2
    freq = 2.0 * np.pi * (np.arange(half) + 0.5) / n

    def forward(at):
        angle = freq[:, None] * at[None, :]
        return np.concatenate([np.cos(angle), -np.sin(angle)], axis=0)

    def inverse(at):
        angle = at[:, None] * freq[None, :]
        return np.concatenate([np.cos(angle), -np.sin(angle)], axis=1) * (2.0 / n)

    ahead = forward(np.arange(n)).astype(np.float32)
    ahead_high = ahead.astype(jnp.bfloat16)
    ahead_low = (ahead - ahead_high.astype(np.float32)).astype(jnp.bfloat16)[:, :taps]
    mixed = inverse(np.arange(rows + EDGE) + behind).astype(jnp.bfloat16)
    back = inverse(np.arange(rows + EDGE)).astype(jnp.bfloat16)
    lags = inverse(np.arange(taps) - behind).astype(jnp.bfloat16)
    return n, ahead_high, ahead_low, mixed, back, lags


def chunks(start, stop, size):
    return [(at, min(size, stop - at)) for at in range(start, stop, size)]


def body(
    n_ctx, length, taps, short, feat, group,
    se, mr, cot, sef, mrf, sfilt, mfilt, decay, ahead, ahead_low, inv_mixed, inv_back, inv_lags,
    out_se, out_mr, out_short, out_medium,
    se_behind, mr_behind, se_after, mr_after, cot_after,
    win, y1, q1, k1, v1, pse, z1, k2, v2, z2,
    hist, up, kspec, gspec, xspec, damp,
    dwide, d2, dz1, d1,
    dks, rs, ag, sks, srs, sag,
    edge_send, edge_recv, hist_send, hist_recv, up_send, up_recv,
    rs_send, rs_recv, ag_send, ag_recv, srs_send, srs_recv, sag_send, sag_recv,
):
    rows, channels = cot.shape
    half = length // 2
    groups = channels // group
    lane_blocks = min(n_ctx, 8)
    row_blocks = n_ctx // lane_blocks
    lane_width = channels // lane_blocks
    piece_rows = taps // row_blocks
    per_group = group // lane_width
    end = rows + EDGE
    up_rows = taps + EDGE
    me = lax.axis_index("ctx")
    has_behind = me > 0
    has_after = me < n_ctx - 1

    barrier = pltpu.get_barrier_semaphore()

    def greet(step, carry):
        pl.semaphore_signal(
            barrier, inc=1, device_id={"ctx": lax.rem(me + step, n_ctx)},
            device_id_type=pl.DeviceIdType.MESH,
        )
        return carry

    lax.fori_loop(1, n_ctx, greet, 0)
    pl.semaphore_wait(barrier, n_ctx - 1)

    def remote(src, dst, send, recv, to):
        return pltpu.make_async_remote_copy(
            src_ref=src, dst_ref=dst, send_sem=send, recv_sem=recv,
            device_id={"ctx": to}, device_id_type=pl.DeviceIdType.MESH,
        )

    last = pl.ds(rows - EDGE, EDGE)
    first = pl.ds(0, EDGE)

    def to_after():
        to = me + 1
        return [
            remote(se.at[:, last, :], se_behind, edge_send.at[0], edge_recv.at[0], to),
            remote(mr.at[:, last, :], mr_behind, edge_send.at[1], edge_recv.at[1], to),
        ]

    def to_behind():
        to = me - 1
        return [
            remote(se.at[:, first, :], se_after, edge_send.at[2], edge_recv.at[2], to),
            remote(mr.at[1, first, :], mr_after, edge_send.at[3], edge_recv.at[3], to),
            remote(cot.at[first, :], cot_after, edge_send.at[4], edge_recv.at[4], to),
        ]

    def hist_copy(i):
        cols = pl.ds(pl.multiple_of(i * group, group), group)
        return remote(
            hist.at[pl.ds(rows, taps), cols], hist.at[pl.ds(0, taps), cols],
            hist_send.at[i], hist_recv.at[i], me + 1,
        )

    def up_copy(i):
        cols = pl.ds(pl.multiple_of(i * group, group), group)
        return remote(
            up.at[pl.ds(0, up_rows), cols], up.at[pl.ds(rows, up_rows), cols],
            up_send.at[i], up_recv.at[i], me - 1,
        )

    @pl.when(has_after)
    def _():
        for copy in to_after():
            copy.start()

    @pl.when(has_behind)
    def _():
        for copy in to_behind():
            copy.start()

    @pl.when(jnp.logical_not(has_behind))
    def _():
        se_behind[...] = jnp.zeros_like(se_behind)
        mr_behind[...] = jnp.zeros_like(mr_behind)
        hist[0:taps, :] = jnp.zeros((taps, channels), BF16)

    @pl.when(jnp.logical_not(has_after))
    def _():
        se_after[...] = jnp.zeros_like(se_after)
        mr_after[...] = jnp.zeros_like(mr_after)
        cot_after[...] = jnp.zeros_like(cot_after)
        up[rows : rows + up_rows, :] = jnp.zeros((up_rows, channels), BF16)

    spare = length - (taps + rows + EDGE)
    if spare:
        hist[length - spare :, :] = jnp.zeros((spare, channels), BF16)
        up[length - spare :, :] = jnp.zeros((spare, channels), BF16)
    win[:, 0:PAD, :] = jnp.zeros((5, PAD, group), F32)
    y1[0:PAD, :] = jnp.zeros((PAD, group), F32)
    pse[0:PAD, :] = jnp.zeros((PAD, channels), F32)
    d2[:, end:, :] = jnp.zeros((3, d2.shape[1] - end, group), F32)
    dz1[end:, :] = jnp.zeros((dz1.shape[0] - end, group), F32)
    sks[...] = jnp.zeros_like(sks)

    def spectra(i, carry):
        cols = pl.ds(pl.multiple_of(i * group, group), group)
        lag = lax.broadcasted_iota(jnp.int32, (taps, group), 0).astype(F32)
        damping = jnp.exp(-lag * decay[:, cols])
        damp[:, cols] = damping
        kernel = mfilt[:, cols] * damping
        high = kernel.astype(BF16)
        low = (kernel - high.astype(F32)).astype(BF16)
        table = ahead[:, 0:taps]
        kspec[:, cols] = (
            jnp.dot(table, high, preferred_element_type=F32)
            + jnp.dot(table, low, preferred_element_type=F32)
            + jnp.dot(ahead_low[...], high, preferred_element_type=F32)
        )
        return carry

    lax.fori_loop(0, groups, spectra, 0)

    @pl.when(has_behind)
    def _():
        for copy in to_after():
            copy.wait_recv()

    @pl.when(has_after)
    def _():
        for copy in to_behind():
            copy.wait_recv()

    def forward(i, carry):
        cols = pl.ds(pl.multiple_of(i * group, group), group)
        for part in range(3):
            win[part, PAD : PAD + EDGE, :] = se_behind[part, :, cols].astype(F32)
            win[part, PAD + EDGE : PAD + EDGE + rows, :] = se[part, :, cols].astype(F32)
            win[part, PAD + EDGE + rows :, :] = se_after[part, :, cols].astype(F32)
        for part in range(2):
            win[3 + part, PAD : PAD + EDGE, :] = mr_behind[part, :, cols].astype(F32)
            win[3 + part, PAD + EDGE : PAD + EDGE + rows, :] = mr[part, :, cols].astype(F32)
        win[4, PAD + EDGE + rows :, :] = mr_after[:, cols].astype(F32)

        def se_mix(part, at, size):
            return sum(
                sef[3 * j + part : 3 * j + part + 1, cols] * win[part, pl.ds(PAD + at - j, size), :]
                for j in range(feat)
            )

        for at, size in [(0, EDGE)] + chunks(EDGE, EDGE + end, 32):
            here = pl.ds(PAD + at, size)
            q = se_mix(0, at, size)
            k = se_mix(1, at, size)
            v = se_mix(2, at, size)
            q1[here, cols] = q
            k1[here, cols] = k
            v1[here, cols] = v
            pse[here, cols] = (k * v).astype(BF16).astype(F32)
            z = sum(
                sfilt[j : j + 1, cols] * pse[pl.ds(PAD + at - j, size), cols] for j in range(short)
            )
            z1[here, cols] = z
            y1[here, :] = (q * z).astype(BF16).astype(F32)
            if at < EDGE:
                continue

            def mr_mix(part):
                return sum(
                    mrf[3 * j + part : 3 * j + part + 1, cols]
                    * (
                        y1[pl.ds(PAD + at - j, size), :]
                        if part == 2
                        else win[3 + part, pl.ds(PAD + at - j, size), :]
                    )
                    for j in range(feat)
                )

            k = mr_mix(1)
            v = mr_mix(2)
            k2[here, cols] = k
            v2[here, cols] = v
            t = at - EDGE
            hist[pl.ds(taps + t, size), cols] = (k * v).astype(BF16)
            if t < rows:
                up[pl.ds(t, size), cols] = (cot[pl.ds(t, size), cols].astype(F32) * mr_mix(0)).astype(BF16)

        @pl.when(has_after)
        def _():
            hist_copy(i).start()

        @pl.when(has_behind)
        def _():
            up_copy(i).start()

        gspec[:, cols] = jnp.dot(ahead[:, 0:rows], up[0:rows, cols], preferred_element_type=F32)
        xspec[:, cols] = jnp.dot(
            ahead[:, taps:length], hist[taps:length, cols], preferred_element_type=F32
        )
        return carry

    lax.fori_loop(0, groups, forward, 0)

    def piece_of(d):
        at_rows = pl.ds(pl.multiple_of((d // lane_blocks) * piece_rows, 16), piece_rows)
        at_cols = pl.ds(pl.multiple_of(lax.rem(d, lane_blocks) * lane_width, lane_width), lane_width)
        return at_rows, at_cols

    def rs_copy(to, slot):
        at_rows, at_cols = piece_of(to)
        return remote(dks.at[at_rows, at_cols], rs.at[slot], rs_send.at[to], rs_recv.at[slot], to)

    def ag_copy(to, slot):
        return remote(ag.at[slot], ag.at[slot], ag_send.at[to], ag_recv.at[slot], to)

    def srs_copy(to, slot):
        _, at_cols = piece_of(to)
        return remote(sks.at[:, at_cols], srs.at[slot], srs_send.at[to], srs_recv.at[slot], to)

    def sag_copy(to, slot):
        return remote(sag.at[slot], sag.at[slot], sag_send.at[to], sag_recv.at[slot], to)

    def for_peers(act):
        def step(s, carry):
            act(lax.rem(me + s, n_ctx))
            return carry

        lax.fori_loop(1, n_ctx, step, 0)

    def medium(i, carry):
        cols = pl.ds(pl.multiple_of(i * group, group), group)

        @pl.when(has_behind)
        def _():
            hist_copy(i).wait_recv()

        x = xspec[:, cols] + jnp.dot(ahead[:, 0:taps], hist[0:taps, cols], preferred_element_type=F32)
        xr, xi = x[:half], x[half:]
        gr, gi = gspec[0:half, cols], gspec[half:, cols]
        lag = jnp.concatenate(
            [(gr * xr + gi * xi).astype(BF16), (gi * xr - gr * xi).astype(BF16)], axis=0
        )
        dks[:, cols] = jnp.dot(inv_lags[...], lag, preferred_element_type=F32).astype(BF16)

        for block in range(per_group):
            for row_block in range(row_blocks):
                owner = row_block * lane_blocks + i * per_group + block

                @pl.when(owner != me)
                def _():
                    rs_copy(owner, me).start()

        kr, ki = kspec[0:half, cols], kspec[half:, cols]
        y = jnp.concatenate(
            [(xr * kr - xi * ki).astype(BF16), (xr * ki + xi * kr).astype(BF16)], axis=0
        )
        z2[:, cols] = jnp.dot(inv_mixed[...], y, preferred_element_type=F32)
        return carry

    lax.fori_loop(0, groups, medium, 0)

    inside = jnp.where(has_after, 1.0, 0.0).astype(F32)

    def backward(i, carry):
        cols = pl.ds(pl.multiple_of(i * group, group), group)

        @pl.when(has_after)
        def _():
            up_copy(i).wait_recv()

        d = gspec[:, cols] + jnp.dot(
            ahead[:, rows:length], up[rows:length, cols], preferred_element_type=F32
        )
        dr, di = d[:half], d[half:]
        kr, ki = kspec[0:half, cols], kspec[half:, cols]
        y = jnp.concatenate(
            [(dr * kr + di * ki).astype(BF16), (di * kr - dr * ki).astype(BF16)], axis=0
        )
        dwide[...] = jnp.dot(inv_back[...], y, preferred_element_type=F32)

        for t, size in chunks(0, end, 32):
            here = pl.ds(t, size)
            there = pl.ds(PAD + EDGE + t, size)
            w = dwide[here, :]
            if t >= rows:
                w = w * inside
                g = cot_after[:, cols].astype(F32)
            else:
                g = cot[here, cols].astype(F32)
            d2[0, here, :] = g * z2[here, cols]
            d2[1, here, :] = w * v2[there, cols]
            d2[2, here, :] = w * k2[there, cols]

        def mr_back(part, t, size):
            return sum(
                mrf[3 * j + part : 3 * j + part + 1, cols] * d2[part, pl.ds(t + j, size), :]
                for j in range(feat)
            )

        for t, size in chunks(0, end, 32):
            here = pl.ds(t, size)
            there = pl.ds(PAD + EDGE + t, size)
            dy = mr_back(2, t, size)
            d1[0, here, :] = dy * z1[there, cols]
            dz1[here, :] = dy * q1[there, cols]
            if t < rows:
                out_mr[0, here, cols] = mr_back(0, t, size).astype(BF16)
                out_mr[1, here, cols] = mr_back(1, t, size).astype(BF16)

        sums = [jnp.zeros((8, group), F32) for _ in range(short)]
        for t, size in chunks(0, end, 32):
            here = pl.ds(t, size)
            there = pl.ds(PAD + EDGE + t, size)
            w = sum(sfilt[j : j + 1, cols] * dz1[pl.ds(t + j, size), :] for j in range(short))
            d1[1, here, :] = w * v1[there, cols]
            d1[2, here, :] = w * k1[there, cols]
            if t < rows:
                dz = dz1[here, :]
                for j in range(short):
                    term = dz * pse[pl.ds(PAD + EDGE + t - j, size), cols]
                    for s in range(0, size, 8):
                        sums[j] = sums[j] + term[s : s + 8]
        for j in range(short):
            sks[j : j + 1, cols] = jnp.sum(sums[j], axis=0, keepdims=True)

        for t, size in chunks(0, rows, 32):
            here = pl.ds(t, size)
            for part in range(3):
                out_se[part, here, cols] = sum(
                    sef[3 * j + part : 3 * j + part + 1, cols] * d1[part, pl.ds(t + j, size), :]
                    for j in range(feat)
                ).astype(BF16)

        @pl.when(i == max(groups - 2, 0))
        def _():
            at_rows, at_cols = piece_of(me)
            rs[me] = dks[at_rows, at_cols]
            for_peers(lambda d: rs_copy(d, d).wait_recv())
            total = rs[0].astype(F32)
            for d in range(1, n_ctx):
                total = total + rs[d].astype(F32)
            ag[me] = total.astype(BF16)
            for_peers(lambda d: ag_copy(d, me).start())

        return carry

    lax.fori_loop(0, groups, backward, 0)

    _, my_cols = piece_of(me)
    for_peers(lambda d: srs_copy(d, me).start())
    srs[me] = sks[:, my_cols]
    scale = 1.0 / math.sqrt(rows * n_ctx)
    for_peers(lambda d: ag_copy(d, d).wait_recv())
    for d in range(n_ctx):
        r, c = (d // lane_blocks) * piece_rows, (d % lane_blocks) * lane_width
        out_medium[r : r + piece_rows, c : c + lane_width] = (
            ag[d].astype(F32) * damp[r : r + piece_rows, c : c + lane_width] * scale
        )
    for_peers(lambda d: srs_copy(d, d).wait_recv())
    total = srs[0]
    for d in range(1, n_ctx):
        total = total + srs[d]
    sag[me] = total * scale
    for_peers(lambda d: sag_copy(d, me).start())

    @pl.when(has_after)
    def _():
        for copy in to_after():
            copy.wait_send()
        for i in range(groups):
            hist_copy(i).wait_send()

    @pl.when(has_behind)
    def _():
        for copy in to_behind():
            copy.wait_send()
        for i in range(groups):
            up_copy(i).wait_send()

    for_peers(lambda d: rs_copy(d, me).wait_send())
    for_peers(lambda d: ag_copy(d, me).wait_send())
    for_peers(lambda d: srs_copy(d, me).wait_send())
    for_peers(lambda d: sag_copy(d, d).wait_recv())
    for d in range(lane_blocks):
        c = d * lane_width
        out_short[:, c : c + lane_width] = sag[d][0:short]
    for_peers(lambda d: sag_copy(d, me).wait_send())


def local(n_ctx, se_input, mr_input, cotangent, se_featurizer, mr_featurizer, se_filter, mr_filter, decay_rate):
    rows, channels = cotangent.shape
    taps, short, feat = mr_filter.shape[0], se_filter.shape[0], se_featurizer.shape[0]
    group = min(256, channels)
    groups = channels // group
    length, ahead, ahead_low, inv_mixed, inv_back, inv_lags = transforms(rows, taps)
    lane_blocks = min(n_ctx, 8)
    lane_width = channels // lane_blocks
    piece_rows = taps // (n_ctx // lane_blocks)
    wide = PAD + EDGE + rows + EDGE
    end = rows + EDGE
    vmem = pltpu.VMEM
    dma = pltpu.SemaphoreType.DMA
    scratch = (
        [vmem((3, EDGE, channels), BF16), vmem((2, EDGE, channels), BF16)]
        + [vmem((3, EDGE, channels), BF16), vmem((EDGE, channels), BF16), vmem((EDGE, channels), BF16)]
        + [vmem((5, wide, group), F32), vmem((wide, group), F32)]
        + [vmem((wide, channels), F32)] * 7
        + [vmem((end, channels), F32)]
        + [vmem((length, channels), BF16)] * 2
        + [vmem((length, channels), F32)] * 3
        + [vmem((taps, channels), F32)]
        + [vmem((end, group), F32), vmem((3, end + 16, group), F32)]
        + [vmem((end + 16, group), F32), vmem((3, end + 16, group), F32)]
        + [vmem((taps, channels), BF16)]
        + [vmem((n_ctx, piece_rows, lane_width), BF16)] * 2
        + [vmem((8, channels), F32)]
        + [vmem((n_ctx, 8, lane_width), F32)] * 2
        + [dma((5,))] * 2
        + [dma((groups,))] * 4
        + [dma((n_ctx,))] * 8
    )
    out_se, out_mr, out_short, out_medium = pl.pallas_call(
        functools.partial(body, n_ctx, length, taps, short, feat, group),
        out_shape=(
            jax.ShapeDtypeStruct((3, rows, channels), BF16),
            jax.ShapeDtypeStruct((2, rows, channels), BF16),
            jax.ShapeDtypeStruct((short, channels), F32),
            jax.ShapeDtypeStruct((taps, channels), F32),
        ),
        in_specs=[pl.BlockSpec(memory_space=pltpu.VMEM)] * 13,
        out_specs=[pl.BlockSpec(memory_space=pltpu.VMEM)] * 4,
        scratch_shapes=scratch,
        compiler_params=pltpu.CompilerParams(
            collective_id=0, has_side_effects=True, vmem_limit_bytes=56 * 1024 * 1024
        ),
        cost_estimate=pl.CostEstimate(
            flops=12 * length * length * channels, bytes_accessed=14 * rows * channels * 2, transcendentals=0
        ),
        name="hyena_pair",
    )(
        jnp.transpose(se_input, (1, 0, 2)),
        jnp.transpose(mr_input, (1, 0, 2)),
        cotangent,
        se_featurizer.reshape(3 * feat, channels),
        mr_featurizer.reshape(3 * feat, channels),
        se_filter,
        mr_filter,
        decay_rate[None, :],
        ahead, ahead_low, inv_mixed, inv_back, inv_lags,
    )
    return jnp.transpose(out_se, (1, 0, 2)), jnp.transpose(out_mr, (1, 0, 2)), out_short, out_medium


def solution(mesh):
    placed = (
        P("ctx", None, "ts"),
        P("ctx", None, "ts"),
        P("ctx", "ts"),
        P(None, None, "ts"),
        P(None, None, "ts"),
        P(None, "ts"),
        P(None, "ts"),
        P("ts"),
    )
    return jax.shard_map(
        functools.partial(local, mesh.shape["ctx"]),
        mesh=mesh,
        in_specs=placed,
        out_specs=(P("ctx", None, "ts"), P("ctx", None, "ts"), P(None, "ts"), P(None, "ts")),
        check_vma=False,
    )
```

```python
import functools
import math

import jax
import jax.numpy as jnp
import numpy as np
from jax import lax
from jax.experimental import pallas as pl
from jax.experimental.pallas import tpu as pltpu
from jax.sharding import PartitionSpec as P

F32 = jnp.float32
BF16 = jnp.bfloat16
EDGE = 16
NEAR = 16
FAR = 48


def round_up(value, unit):
    return -(-value // unit) * unit


def transforms(rows, taps):
    behind = taps
    span = behind + rows + EDGE
    n = round_up(span, 32)
    half = n // 2
    freq = 2.0 * np.pi * (np.arange(half) + 0.5) / n

    def forward(at):
        angle = freq[:, None] * at[None, :]
        return np.concatenate([np.cos(angle), -np.sin(angle)], axis=0)

    def inverse(at):
        angle = at[:, None] * freq[None, :]
        return np.concatenate([np.cos(angle), -np.sin(angle)], axis=1) * (2.0 / n)

    ahead = forward(np.arange(n)).astype(np.float32)
    ahead_high = ahead.astype(jnp.bfloat16)
    ahead_low = (ahead - ahead_high.astype(np.float32)).astype(jnp.bfloat16)[:, :taps]
    wide = rows + 2 * EDGE
    place = (np.arange(wide) % 8) * (wide // 8) + np.arange(wide) // 8
    weave = (place[:, None] == np.arange(wide)[None, :]).astype(jnp.bfloat16)
    unweave = np.ascontiguousarray(weave.T[EDGE : EDGE + rows])
    at = place - EDGE
    from_hist = np.where(at >= 0, ahead[:, np.maximum(behind + at, 0)], 0.0).astype(jnp.bfloat16)
    own = (at >= 0) & (at < rows)
    from_up = np.where(own, ahead[:, np.clip(at, 0, rows)], 0.0).astype(jnp.bfloat16)
    mixed = inverse(at + behind).astype(jnp.bfloat16)
    back = inverse(at).astype(jnp.bfloat16)
    lags = inverse(np.arange(taps) - behind).astype(jnp.bfloat16)
    return n, (ahead_high, ahead_low, from_hist, from_up, mixed, back, lags, weave, unweave)


def chunks(start, stop, size):
    return [(at, min(size, stop - at)) for at in range(start, stop, size)]


def body(
    n_ctx, length, taps, short, feat, group,
    se, mr, cot, sef, mrf, sfilt, mfilt, decay, ahead, ahead_low, from_hist, from_up, inv_mixed, inv_back, inv_lags, weave, unweave,
    out_se, out_mr, out_short, out_medium,
    se_behind, mr_behind, se_after, mr_after, cot_after,
    win, y1, q1, k1, v1, pse, z1, k2, v2, z2, upstream,
    hist_in, hist_out, up_in, up_out, product, raised, inner, alive, outgoing, kspec, gspec, xspec, damp,
    dwide, d2, dz1, d1,
    dks, rs, ag, sks, srs, sag,
    edge_send, edge_recv, hist_send, hist_recv, up_send, up_recv,
    rs_send, rs_recv, ag_send, ag_recv, srs_send, srs_recv, sag_send, sag_recv,
):
    rows, channels = cot.shape
    half = length // 2
    groups = channels // group
    lane_blocks = min(n_ctx, 8)
    row_blocks = n_ctx // lane_blocks
    lane_width = channels // lane_blocks
    piece_rows = taps // row_blocks
    per_group = group // lane_width
    wide = rows + 2 * EDGE
    up_rows = taps + EDGE
    me = lax.axis_index("ctx")
    has_behind = me > 0
    has_after = me < n_ctx - 1

    barrier = pltpu.get_barrier_semaphore()

    def greet(step, carry):
        pl.semaphore_signal(
            barrier, inc=1, device_id={"ctx": lax.rem(me + step, n_ctx)},
            device_id_type=pl.DeviceIdType.MESH,
        )
        return carry

    lax.fori_loop(1, n_ctx, greet, 0)
    pl.semaphore_wait(barrier, n_ctx - 1)

    def remote(src, dst, send, recv, to):
        return pltpu.make_async_remote_copy(
            src_ref=src, dst_ref=dst, send_sem=send, recv_sem=recv,
            device_id={"ctx": to}, device_id_type=pl.DeviceIdType.MESH,
        )

    last = pl.ds(rows - EDGE, EDGE)
    first = pl.ds(0, EDGE)

    def to_after():
        to = me + 1
        return [
            remote(se.at[:, last, :], se_behind, edge_send.at[0], edge_recv.at[0], to),
            remote(mr.at[:, last, :], mr_behind, edge_send.at[1], edge_recv.at[1], to),
        ]

    def to_behind():
        to = me - 1
        return [
            remote(se.at[:, first, :], se_after, edge_send.at[2], edge_recv.at[2], to),
            remote(mr.at[1, first, :], mr_after, edge_send.at[3], edge_recv.at[3], to),
            remote(cot.at[first, :], cot_after, edge_send.at[4], edge_recv.at[4], to),
        ]

    def hist_copy(i):
        cols = pl.ds(pl.multiple_of(i * group, group), group)
        return remote(
            hist_out.at[:, cols], hist_in.at[:, cols],
            hist_send.at[i], hist_recv.at[i], me + 1,
        )

    def up_copy(i):
        cols = pl.ds(pl.multiple_of(i * group, group), group)
        return remote(
            up_out.at[:, cols], up_in.at[pl.ds(0, up_rows), cols],
            up_send.at[i], up_recv.at[i], me - 1,
        )

    @pl.when(has_after)
    def _():
        for copy in to_after():
            copy.start()

    @pl.when(has_behind)
    def _():
        for copy in to_behind():
            copy.start()

    @pl.when(jnp.logical_not(has_behind))
    def _():
        se_behind[...] = jnp.zeros_like(se_behind)
        mr_behind[...] = jnp.zeros_like(mr_behind)
        hist_in[...] = jnp.zeros_like(hist_in)

    @pl.when(jnp.logical_not(has_after))
    def _():
        se_after[...] = jnp.zeros_like(se_after)
        mr_after[...] = jnp.zeros_like(mr_after)
        cot_after[...] = jnp.zeros_like(cot_after)
        up_in[0:up_rows, :] = jnp.zeros((up_rows, channels), BF16)

    spare = length - rows - up_rows
    if spare:
        up_in[up_rows:, :] = jnp.zeros((spare, channels), BF16)
    sks[...] = jnp.zeros_like(sks)
    at_row = lax.broadcasted_iota(jnp.int32, (wide, group), 0)
    placed = lax.rem(at_row, 8) * (wide // 8) + at_row // 8
    inside = jnp.where(has_after, 1.0, 0.0).astype(F32)
    inner[...] = jnp.where((placed >= EDGE) & (placed < EDGE + rows), 1.0, 0.0).astype(F32)
    alive[...] = jnp.where(placed >= EDGE + rows, inside, 1.0).astype(F32)

    def spectra(i, carry):
        cols = pl.ds(pl.multiple_of(i * group, group), group)
        lag = lax.broadcasted_iota(jnp.int32, (taps, group), 0).astype(F32)
        damping = jnp.exp(-lag * decay[:, cols])
        damp[:, cols] = damping
        kernel = mfilt[:, cols] * damping
        high = kernel.astype(BF16)
        low = (kernel - high.astype(F32)).astype(BF16)
        table = ahead[:, 0:taps]
        kspec[:, cols] = (
            jnp.dot(table, high, preferred_element_type=F32)
            + jnp.dot(table, low, preferred_element_type=F32)
            + jnp.dot(ahead_low[...], high, preferred_element_type=F32)
        )
        return carry

    lax.fori_loop(0, groups, spectra, 0)

    @pl.when(has_behind)
    def _():
        for copy in to_after():
            copy.wait_recv()

    @pl.when(has_after)
    def _():
        for copy in to_behind():
            copy.wait_recv()

    def forward(i, carry):
        cols = pl.ds(pl.multiple_of(i * group, group), group)
        blank = jnp.zeros((EDGE, group), BF16)

        def woven(*pieces):
            return jnp.dot(weave[...], jnp.concatenate(pieces, axis=0), preferred_element_type=F32)

        for part in range(3):
            win[part, NEAR:, :] = woven(se_behind[part, :, cols], se[part, :, cols], se_after[part, :, cols])
        win[3, NEAR:, :] = woven(mr_behind[0, :, cols], mr[0, :, cols], blank)
        win[4, NEAR:, :] = woven(mr_behind[1, :, cols], mr[1, :, cols], mr_after[:, cols])
        upstream[:, cols] = woven(blank, cot[:, cols], cot_after[:, cols])
        for part in range(5):
            win[part, 0:NEAR, :] = win[part, wide - 1 : wide + NEAR - 1, :]

        def se_mix(part, at, size):
            return sum(
                sef[j, part : part + 1, cols] * win[part, pl.ds(NEAR + at - 8 * j, size), :]
                for j in range(feat)
            )

        for at, size in chunks(0, wide, 32):
            here = pl.ds(at, size)
            k = se_mix(1, at, size)
            v = se_mix(2, at, size)
            q1[here, cols] = se_mix(0, at, size)
            k1[here, cols] = k
            v1[here, cols] = v
            pse[pl.ds(FAR + at, size), cols] = (k * v).astype(BF16).astype(F32)
        pse[0:FAR, cols] = pse[wide - 1 : wide + FAR - 1, cols]

        for at, size in chunks(0, wide, 32):
            here = pl.ds(at, size)
            z = sum(
                sfilt[j : j + 1, cols] * pse[pl.ds(FAR + at - 8 * j, size), cols] for j in range(short)
            )
            z1[here, cols] = z
            y1[pl.ds(NEAR + at, size), :] = (q1[here, cols] * z).astype(BF16).astype(F32)
        y1[0:NEAR, :] = y1[wide - 1 : wide + NEAR - 1, :]

        for at, size in chunks(0, wide, 32):
            here = pl.ds(at, size)

            def mr_mix(part):
                return sum(
                    mrf[j, part : part + 1, cols]
                    * (
                        y1[pl.ds(NEAR + at - 8 * j, size), :]
                        if part == 2
                        else win[3 + part, pl.ds(NEAR + at - 8 * j, size), :]
                    )
                    for j in range(feat)
                )

            k = mr_mix(1)
            v = mr_mix(2)
            k2[here, cols] = k
            v2[here, cols] = v
            product[here, :] = (k * v).astype(BF16)
            raised[here, :] = (upstream[here, cols] * mr_mix(0)).astype(BF16)

        hist_out[:, cols] = jnp.dot(
            unweave[rows - taps : rows, :], product[...], preferred_element_type=F32
        ).astype(BF16)
        up_out[:, cols] = jnp.dot(
            unweave[0:up_rows, :], raised[...], preferred_element_type=F32
        ).astype(BF16)

        @pl.when(has_after)
        def _():
            hist_copy(i).start()

        @pl.when(has_behind)
        def _():
            up_copy(i).start()

        gspec[:, cols] = jnp.dot(from_up[...], raised[...], preferred_element_type=F32)
        xspec[:, cols] = jnp.dot(from_hist[...], product[...], preferred_element_type=F32)
        return carry

    lax.fori_loop(0, groups, forward, 0)

    def piece_of(d):
        at_rows = pl.ds(pl.multiple_of((d // lane_blocks) * piece_rows, 16), piece_rows)
        at_cols = pl.ds(pl.multiple_of(lax.rem(d, lane_blocks) * lane_width, lane_width), lane_width)
        return at_rows, at_cols

    def rs_copy(to, slot):
        at_rows, at_cols = piece_of(to)
        return remote(dks.at[at_rows, at_cols], rs.at[slot], rs_send.at[to], rs_recv.at[slot], to)

    def ag_copy(to, slot):
        return remote(ag.at[slot], ag.at[slot], ag_send.at[to], ag_recv.at[slot], to)

    def srs_copy(to, slot):
        _, at_cols = piece_of(to)
        return remote(sks.at[:, at_cols], srs.at[slot], srs_send.at[to], srs_recv.at[slot], to)

    def sag_copy(to, slot):
        return remote(sag.at[slot], sag.at[slot], sag_send.at[to], sag_recv.at[slot], to)

    def for_peers(act):
        def step(s, carry):
            act(lax.rem(me + s, n_ctx))
            return carry

        lax.fori_loop(1, n_ctx, step, 0)

    def medium(i, carry):
        cols = pl.ds(pl.multiple_of(i * group, group), group)

        @pl.when(has_behind)
        def _():
            hist_copy(i).wait_recv()

        x = xspec[:, cols] + jnp.dot(ahead[:, 0:taps], hist_in[:, cols], preferred_element_type=F32)
        xr, xi = x[:half], x[half:]
        gr, gi = gspec[0:half, cols], gspec[half:, cols]
        lag = jnp.concatenate(
            [(gr * xr + gi * xi).astype(BF16), (gi * xr - gr * xi).astype(BF16)], axis=0
        )
        dks[:, cols] = jnp.dot(inv_lags[...], lag, preferred_element_type=F32).astype(BF16)

        for block in range(per_group):
            for row_block in range(row_blocks):
                owner = row_block * lane_blocks + i * per_group + block

                @pl.when(owner != me)
                def _():
                    rs_copy(owner, me).start()

        kr, ki = kspec[0:half, cols], kspec[half:, cols]
        y = jnp.concatenate(
            [(xr * kr - xi * ki).astype(BF16), (xr * ki + xi * kr).astype(BF16)], axis=0
        )
        z2[:, cols] = jnp.dot(inv_mixed[...], y, preferred_element_type=F32)
        return carry

    lax.fori_loop(0, groups, medium, 0)

    def backward(i, carry):
        cols = pl.ds(pl.multiple_of(i * group, group), group)

        @pl.when(has_after)
        def _():
            up_copy(i).wait_recv()

        d = gspec[:, cols] + jnp.dot(
            ahead[:, rows:length], up_in[:, cols], preferred_element_type=F32
        )
        dr, di = d[:half], d[half:]
        kr, ki = kspec[0:half, cols], kspec[half:, cols]
        y = jnp.concatenate(
            [(dr * kr + di * ki).astype(BF16), (di * kr - dr * ki).astype(BF16)], axis=0
        )
        dwide[...] = jnp.dot(inv_back[...], y, preferred_element_type=F32)

        for t, size in chunks(0, wide, 32):
            here = pl.ds(t, size)
            w = dwide[here, :] * alive[here, :]
            d2[0, here, :] = upstream[here, cols] * z2[here, cols]
            d2[1, here, :] = w * v2[here, cols]
            d2[2, here, :] = w * k2[here, cols]
        for part in range(3):
            d2[part, wide:, :] = d2[part, 1 : NEAR + 1, :]

        def mr_back(part, t, size):
            return sum(
                mrf[j, part : part + 1, cols] * d2[part, pl.ds(t + 8 * j, size), :]
                for j in range(feat)
            )

        for t, size in chunks(0, wide, 32):
            here = pl.ds(t, size)
            dy = mr_back(2, t, size)
            d1[0, here, :] = dy * z1[here, cols]
            dz1[here, :] = dy * q1[here, cols]
            outgoing[0, here, :] = mr_back(0, t, size).astype(BF16)
            outgoing[1, here, :] = mr_back(1, t, size).astype(BF16)
        dz1[wide:, :] = dz1[1 : FAR + 1, :]
        for part in range(2):
            out_mr[part, :, cols] = jnp.dot(
                unweave[...], outgoing[part], preferred_element_type=F32
            ).astype(BF16)

        sums = [jnp.zeros((8, group), F32) for _ in range(short)]
        for t, size in chunks(0, wide, 32):
            here = pl.ds(t, size)
            w = sum(sfilt[j : j + 1, cols] * dz1[pl.ds(t + 8 * j, size), :] for j in range(short))
            d1[1, here, :] = w * v1[here, cols]
            d1[2, here, :] = w * k1[here, cols]
            dz = dz1[here, :] * inner[here, :]
            for j in range(short):
                term = dz * pse[pl.ds(FAR + t - 8 * j, size), cols]
                for s in range(0, size, 8):
                    sums[j] = sums[j] + term[s : s + 8]
        for j in range(short):
            sks[j : j + 1, cols] = jnp.sum(sums[j], axis=0, keepdims=True)
        for part in range(3):
            d1[part, wide:, :] = d1[part, 1 : NEAR + 1, :]

        for part in range(3):
            for t, size in chunks(0, wide, 32):
                outgoing[2 + part, pl.ds(t, size), :] = sum(
                    sef[j, part : part + 1, cols] * d1[part, pl.ds(t + 8 * j, size), :]
                    for j in range(feat)
                ).astype(BF16)
            out_se[part, :, cols] = jnp.dot(
                unweave[...], outgoing[2 + part], preferred_element_type=F32
            ).astype(BF16)

        @pl.when(i == max(groups - 2, 0))
        def _():
            at_rows, at_cols = piece_of(me)
            rs[me] = dks[at_rows, at_cols]
            for_peers(lambda d: rs_copy(d, d).wait_recv())
            total = rs[0].astype(F32)
            for d in range(1, n_ctx):
                total = total + rs[d].astype(F32)
            ag[me] = total.astype(BF16)
            for_peers(lambda d: ag_copy(d, me).start())

        return carry

    lax.fori_loop(0, groups, backward, 0)

    _, my_cols = piece_of(me)
    for_peers(lambda d: srs_copy(d, me).start())
    srs[me] = sks[:, my_cols]
    scale = 1.0 / math.sqrt(rows * n_ctx)
    for_peers(lambda d: ag_copy(d, d).wait_recv())
    for d in range(n_ctx):
        r, c = (d // lane_blocks) * piece_rows, (d % lane_blocks) * lane_width
        out_medium[r : r + piece_rows, c : c + lane_width] = (
            ag[d].astype(F32) * damp[r : r + piece_rows, c : c + lane_width] * scale
        )
    for_peers(lambda d: srs_copy(d, d).wait_recv())
    total = srs[0]
    for d in range(1, n_ctx):
        total = total + srs[d]
    sag[me] = total * scale
    for_peers(lambda d: sag_copy(d, me).start())

    @pl.when(has_after)
    def _():
        for copy in to_after():
            copy.wait_send()
        for i in range(groups):
            hist_copy(i).wait_send()

    @pl.when(has_behind)
    def _():
        for copy in to_behind():
            copy.wait_send()
        for i in range(groups):
            up_copy(i).wait_send()

    for_peers(lambda d: rs_copy(d, me).wait_send())
    for_peers(lambda d: ag_copy(d, me).wait_send())
    for_peers(lambda d: srs_copy(d, me).wait_send())
    for_peers(lambda d: sag_copy(d, d).wait_recv())
    for d in range(lane_blocks):
        c = d * lane_width
        out_short[:, c : c + lane_width] = sag[d][0:short]
    for_peers(lambda d: sag_copy(d, me).wait_send())


def local(n_ctx, se_input, mr_input, cotangent, se_featurizer, mr_featurizer, se_filter, mr_filter, decay_rate):
    rows, channels = cotangent.shape
    taps, short, feat = mr_filter.shape[0], se_filter.shape[0], se_featurizer.shape[0]
    group = min(256, channels)
    groups = channels // group
    length, tables = transforms(rows, taps)
    lane_blocks = min(n_ctx, 8)
    lane_width = channels // lane_blocks
    piece_rows = taps // (n_ctx // lane_blocks)
    wide = rows + 2 * EDGE
    vmem = pltpu.VMEM
    dma = pltpu.SemaphoreType.DMA
    scratch = (
        [vmem((3, EDGE, channels), BF16), vmem((2, EDGE, channels), BF16)]
        + [vmem((3, EDGE, channels), BF16), vmem((EDGE, channels), BF16), vmem((EDGE, channels), BF16)]
        + [vmem((5, NEAR + wide, group), F32), vmem((NEAR + wide, group), F32)]
        + [vmem((wide, channels), F32)] * 3
        + [vmem((FAR + wide, channels), F32)]
        + [vmem((wide, channels), F32)] * 5
        + [vmem((taps, channels), BF16)] * 2
        + [vmem((length - rows, channels), BF16), vmem((taps + EDGE, channels), BF16)]
        + [vmem((wide, group), BF16)] * 2
        + [vmem((wide, group), F32)] * 2
        + [vmem((5, wide, group), BF16)]
        + [vmem((length, channels), F32)] * 3
        + [vmem((taps, channels), F32)]
        + [vmem((wide, group), F32), vmem((3, wide + NEAR, group), F32)]
        + [vmem((wide + FAR, group), F32), vmem((3, wide + NEAR, group), F32)]
        + [vmem((taps, channels), BF16)]
        + [vmem((n_ctx, piece_rows, lane_width), BF16)] * 2
        + [vmem((8, channels), F32)]
        + [vmem((n_ctx, 8, lane_width), F32)] * 2
        + [dma((5,))] * 2
        + [dma((groups,))] * 4
        + [dma((n_ctx,))] * 8
    )
    out_se, out_mr, out_short, out_medium = pl.pallas_call(
        functools.partial(body, n_ctx, length, taps, short, feat, group),
        out_shape=(
            jax.ShapeDtypeStruct((3, rows, channels), BF16),
            jax.ShapeDtypeStruct((2, rows, channels), BF16),
            jax.ShapeDtypeStruct((short, channels), F32),
            jax.ShapeDtypeStruct((taps, channels), F32),
        ),
        in_specs=[pl.BlockSpec(memory_space=pltpu.VMEM)] * (8 + len(tables)),
        out_specs=[pl.BlockSpec(memory_space=pltpu.VMEM)] * 4,
        scratch_shapes=scratch,
        compiler_params=pltpu.CompilerParams(
            collective_id=0, has_side_effects=True, vmem_limit_bytes=56 * 1024 * 1024
        ),
        cost_estimate=pl.CostEstimate(
            flops=12 * length * length * channels, bytes_accessed=14 * rows * channels * 2, transcendentals=0
        ),
        name="hyena_pair",
    )(
        jnp.transpose(se_input, (1, 0, 2)),
        jnp.transpose(mr_input, (1, 0, 2)),
        cotangent,
        se_featurizer,
        mr_featurizer,
        se_filter,
        mr_filter,
        decay_rate[None, :],
        *tables,
    )
    return jnp.transpose(out_se, (1, 0, 2)), jnp.transpose(out_mr, (1, 0, 2)), out_short, out_medium


def solution(mesh):
    placed = (
        P("ctx", None, "ts"),
        P("ctx", None, "ts"),
        P("ctx", "ts"),
        P(None, None, "ts"),
        P(None, None, "ts"),
        P(None, "ts"),
        P(None, "ts"),
        P("ts"),
    )
    return jax.shard_map(
        functools.partial(local, mesh.shape["ctx"]),
        mesh=mesh,
        in_specs=placed,
        out_specs=(P("ctx", None, "ts"), P("ctx", None, "ts"), P(None, "ts"), P(None, "ts")),
        check_vma=False,
    )
```

```python
import functools
import math

import jax
import jax.numpy as jnp
import numpy as np
from jax import lax
from jax.experimental import pallas as pl
from jax.experimental.pallas import tpu as pltpu
from jax.sharding import PartitionSpec as P

F32 = jnp.float32
BF16 = jnp.bfloat16
EDGE = 16
NEAR = 16
FAR = 48


def round_up(value, unit):
    return -(-value // unit) * unit


def transforms(rows, taps):
    behind = taps
    span = behind + rows + EDGE
    n = round_up(span, 32)
    half = n // 2
    freq = 2.0 * np.pi * (np.arange(half) + 0.5) / n

    def forward(at):
        angle = freq[:, None] * at[None, :]
        return np.concatenate([np.cos(angle), -np.sin(angle)], axis=0)

    def inverse(at):
        angle = at[:, None] * freq[None, :]
        return np.concatenate([np.cos(angle), -np.sin(angle)], axis=1) * (2.0 / n)

    ahead = forward(np.arange(n)).astype(np.float32)
    ahead_high = ahead.astype(jnp.bfloat16)
    ahead_low = (ahead - ahead_high.astype(np.float32)).astype(jnp.bfloat16)[:, :taps]
    wide = rows + 2 * EDGE
    place = (np.arange(wide) % 8) * (wide // 8) + np.arange(wide) // 8
    weave = (place[:, None] == np.arange(wide)[None, :]).astype(jnp.bfloat16)
    unweave = np.ascontiguousarray(weave.T[EDGE : EDGE + rows])
    at = place - EDGE
    from_hist = np.where(at >= 0, ahead[:, np.maximum(behind + at, 0)], 0.0).astype(jnp.bfloat16)
    own = (at >= 0) & (at < rows)
    from_up = np.where(own, ahead[:, np.clip(at, 0, rows)], 0.0).astype(jnp.bfloat16)
    mixed = inverse(at + behind).astype(jnp.bfloat16)
    back = inverse(at).astype(jnp.bfloat16)
    lags = inverse(np.arange(taps) - behind).astype(jnp.bfloat16)
    return n, (ahead_high, ahead_low, from_hist, from_up, mixed, back, lags, weave, unweave)


def chunks(start, stop, size):
    return [(at, min(size, stop - at)) for at in range(start, stop, size)]


def body(
    n_ctx, length, taps, short, feat, group,
    se_far, mr_far, cot_far, sef, mrf, sfilt, mfilt, decay, ahead, ahead_low,
    from_hist_far, from_up_far, inv_mixed_far, inv_back_far, inv_lags_far, weave_far, unweave_far,
    out_se, out_mr, out_short, out_medium,
    se_behind, mr_behind, se_after, mr_after, cot_after,
    win, y1, q1, k1, v1, pse, z1, k2, v2, z2, upstream,
    hist_in, hist_out, up_in, up_out, product, raised, inner, alive, outgoing, kspec, gspec, xspec, damp,
    dwide, d2, dz1, d1,
    dks, rs, ag, sks, srs, sag,
    edge_send, edge_recv, hist_send, hist_recv, up_send, up_recv,
    rs_send, rs_recv, ag_send, ag_recv, srs_send, srs_recv, sag_send, sag_recv,
    se, mr, cot, from_hist, from_up, inv_mixed, inv_back, inv_lags, weave, unweave, load_sem,
):
    rows, channels = cot_far.shape
    half = length // 2
    groups = channels // group
    lane_blocks = min(n_ctx, 8)
    row_blocks = n_ctx // lane_blocks
    lane_width = channels // lane_blocks
    piece_rows = taps // row_blocks
    per_group = group // lane_width
    wide = rows + 2 * EDGE
    up_rows = taps + EDGE
    me = lax.axis_index("ctx")
    has_behind = me > 0
    has_after = me < n_ctx - 1

    far = (
        se_far, mr_far, cot_far, weave_far, from_hist_far, from_up_far, unweave_far,
        inv_lags_far, inv_mixed_far, inv_back_far,
    )
    close = (se, mr, cot, weave, from_hist, from_up, unweave, inv_lags, inv_mixed, inv_back)
    loads = [
        pltpu.make_async_copy(src, dst, load_sem.at[at])
        for at, (src, dst) in enumerate(zip(far, close))
    ]
    for load in loads:
        load.start()

    barrier = pltpu.get_barrier_semaphore()

    def greet(step, carry):
        pl.semaphore_signal(
            barrier, inc=1, device_id={"ctx": lax.rem(me + step, n_ctx)},
            device_id_type=pl.DeviceIdType.MESH,
        )
        return carry

    lax.fori_loop(1, n_ctx, greet, 0)
    pl.semaphore_wait(barrier, n_ctx - 1)

    def remote(src, dst, send, recv, to):
        return pltpu.make_async_remote_copy(
            src_ref=src, dst_ref=dst, send_sem=send, recv_sem=recv,
            device_id={"ctx": to}, device_id_type=pl.DeviceIdType.MESH,
        )

    last = pl.ds(rows - EDGE, EDGE)
    first = pl.ds(0, EDGE)

    def to_after(i):
        to = me + 1
        cols = pl.ds(pl.multiple_of(i * group, group), group)
        pairs = [
            (se_far.at[:, last, cols], se_behind.at[:, :, cols]),
            (mr_far.at[:, last, cols], mr_behind.at[:, :, cols]),
        ]
        return [
            remote(src, dst, edge_send.at[at, i], edge_recv.at[at, i], to)
            for at, (src, dst) in enumerate(pairs)
        ]

    def to_behind(i):
        to = me - 1
        cols = pl.ds(pl.multiple_of(i * group, group), group)
        pairs = [
            (se_far.at[:, first, cols], se_after.at[:, :, cols]),
            (mr_far.at[1, first, cols], mr_after.at[:, cols]),
            (cot_far.at[first, cols], cot_after.at[:, cols]),
        ]
        return [
            remote(src, dst, edge_send.at[2 + at, i], edge_recv.at[2 + at, i], to)
            for at, (src, dst) in enumerate(pairs)
        ]

    def hist_copy(i):
        cols = pl.ds(pl.multiple_of(i * group, group), group)
        return remote(
            hist_out.at[:, cols], hist_in.at[:, cols],
            hist_send.at[i], hist_recv.at[i], me + 1,
        )

    def up_copy(i):
        cols = pl.ds(pl.multiple_of(i * group, group), group)
        return remote(
            up_out.at[:, cols], up_in.at[pl.ds(0, up_rows), cols],
            up_send.at[i], up_recv.at[i], me - 1,
        )

    for i in range(groups):

        @pl.when(has_after)
        def _():
            for copy in to_after(i):
                copy.start()

        @pl.when(has_behind)
        def _():
            for copy in to_behind(i):
                copy.start()

    @pl.when(jnp.logical_not(has_behind))
    def _():
        se_behind[...] = jnp.zeros_like(se_behind)
        mr_behind[...] = jnp.zeros_like(mr_behind)
        hist_in[...] = jnp.zeros_like(hist_in)

    @pl.when(jnp.logical_not(has_after))
    def _():
        se_after[...] = jnp.zeros_like(se_after)
        mr_after[...] = jnp.zeros_like(mr_after)
        cot_after[...] = jnp.zeros_like(cot_after)
        up_in[0:up_rows, :] = jnp.zeros((up_rows, channels), BF16)

    spare = length - rows - up_rows
    if spare:
        up_in[up_rows:, :] = jnp.zeros((spare, channels), BF16)
    sks[...] = jnp.zeros_like(sks)
    at_row = lax.broadcasted_iota(jnp.int32, (wide, group), 0)
    placed = lax.rem(at_row, 8) * (wide // 8) + at_row // 8
    inside = jnp.where(has_after, 1.0, 0.0).astype(F32)
    inner[...] = jnp.where((placed >= EDGE) & (placed < EDGE + rows), 1.0, 0.0).astype(F32)
    alive[...] = jnp.where(placed >= EDGE + rows, inside, 1.0).astype(F32)

    def spectra(i, carry):
        cols = pl.ds(pl.multiple_of(i * group, group), group)
        lag = lax.broadcasted_iota(jnp.int32, (taps, group), 0).astype(F32)
        damping = jnp.exp(-lag * decay[:, cols])
        damp[:, cols] = damping
        kernel = mfilt[:, cols] * damping
        high = kernel.astype(BF16)
        low = (kernel - high.astype(F32)).astype(BF16)
        table = ahead[:, 0:taps]
        kspec[:, cols] = (
            jnp.dot(table, high, preferred_element_type=F32)
            + jnp.dot(table, low, preferred_element_type=F32)
            + jnp.dot(ahead_low[...], high, preferred_element_type=F32)
        )
        return carry

    lax.fori_loop(0, groups, spectra, 0)

    for load in loads:
        load.wait()

    def forward(i, carry):
        cols = pl.ds(pl.multiple_of(i * group, group), group)

        @pl.when(has_behind)
        def _():
            for copy in to_after(i):
                copy.wait_recv()

        @pl.when(has_after)
        def _():
            for copy in to_behind(i):
                copy.wait_recv()

        blank = jnp.zeros((EDGE, group), BF16)

        def woven(*pieces):
            return jnp.dot(weave[...], jnp.concatenate(pieces, axis=0), preferred_element_type=F32)

        for part in range(3):
            win[part, NEAR:, :] = woven(se_behind[part, :, cols], se[part, :, cols], se_after[part, :, cols])
        win[3, NEAR:, :] = woven(mr_behind[0, :, cols], mr[0, :, cols], blank)
        win[4, NEAR:, :] = woven(mr_behind[1, :, cols], mr[1, :, cols], mr_after[:, cols])
        upstream[:, cols] = woven(blank, cot[:, cols], cot_after[:, cols])
        for part in range(5):
            win[part, 0:NEAR, :] = win[part, wide - 1 : wide + NEAR - 1, :]

        def se_mix(part, at, size):
            return sum(
                sef[j, part : part + 1, cols] * win[part, pl.ds(NEAR + at - 8 * j, size), :]
                for j in range(feat)
            )

        for at, size in chunks(0, wide, 32):
            here = pl.ds(at, size)
            k = se_mix(1, at, size)
            v = se_mix(2, at, size)
            q1[here, cols] = se_mix(0, at, size)
            k1[here, cols] = k
            v1[here, cols] = v
            pse[pl.ds(FAR + at, size), cols] = (k * v).astype(BF16).astype(F32)
        pse[0:FAR, cols] = pse[wide - 1 : wide + FAR - 1, cols]

        for at, size in chunks(0, wide, 32):
            here = pl.ds(at, size)
            z = sum(
                sfilt[j : j + 1, cols] * pse[pl.ds(FAR + at - 8 * j, size), cols] for j in range(short)
            )
            z1[here, cols] = z
            y1[pl.ds(NEAR + at, size), :] = (q1[here, cols] * z).astype(BF16).astype(F32)
        y1[0:NEAR, :] = y1[wide - 1 : wide + NEAR - 1, :]

        for at, size in chunks(0, wide, 32):
            here = pl.ds(at, size)

            def mr_mix(part):
                return sum(
                    mrf[j, part : part + 1, cols]
                    * (
                        y1[pl.ds(NEAR + at - 8 * j, size), :]
                        if part == 2
                        else win[3 + part, pl.ds(NEAR + at - 8 * j, size), :]
                    )
                    for j in range(feat)
                )

            k = mr_mix(1)
            v = mr_mix(2)
            k2[here, cols] = k
            v2[here, cols] = v
            product[here, :] = (k * v).astype(BF16)
            raised[here, :] = (upstream[here, cols] * mr_mix(0)).astype(BF16)

        hist_out[:, cols] = jnp.dot(
            unweave[rows - taps : rows, :], product[...], preferred_element_type=F32
        ).astype(BF16)
        up_out[:, cols] = jnp.dot(
            unweave[0:up_rows, :], raised[...], preferred_element_type=F32
        ).astype(BF16)

        @pl.when(has_after)
        def _():
            hist_copy(i).start()

        @pl.when(has_behind)
        def _():
            up_copy(i).start()

        gspec[:, cols] = jnp.dot(from_up[...], raised[...], preferred_element_type=F32)
        xspec[:, cols] = jnp.dot(from_hist[...], product[...], preferred_element_type=F32)
        return carry

    lax.fori_loop(0, groups, forward, 0)

    def piece_of(d):
        at_rows = pl.ds(pl.multiple_of((d // lane_blocks) * piece_rows, 16), piece_rows)
        at_cols = pl.ds(pl.multiple_of(lax.rem(d, lane_blocks) * lane_width, lane_width), lane_width)
        return at_rows, at_cols

    def rs_copy(to, slot):
        at_rows, at_cols = piece_of(to)
        return remote(dks.at[at_rows, at_cols], rs.at[slot], rs_send.at[to], rs_recv.at[slot], to)

    def ag_copy(to, slot):
        return remote(ag.at[slot], ag.at[slot], ag_send.at[to], ag_recv.at[slot], to)

    def srs_copy(to, slot):
        _, at_cols = piece_of(to)
        return remote(sks.at[:, at_cols], srs.at[slot], srs_send.at[to], srs_recv.at[slot], to)

    def sag_copy(to, slot):
        return remote(sag.at[slot], sag.at[slot], sag_send.at[to], sag_recv.at[slot], to)

    def for_peers(act):
        def step(s, carry):
            act(lax.rem(me + s, n_ctx))
            return carry

        lax.fori_loop(1, n_ctx, step, 0)

    def medium(i, carry):
        cols = pl.ds(pl.multiple_of(i * group, group), group)

        @pl.when(has_behind)
        def _():
            hist_copy(i).wait_recv()

        x = xspec[:, cols] + jnp.dot(ahead[:, 0:taps], hist_in[:, cols], preferred_element_type=F32)
        xr, xi = x[:half], x[half:]
        gr, gi = gspec[0:half, cols], gspec[half:, cols]
        lag = jnp.concatenate(
            [(gr * xr + gi * xi).astype(BF16), (gi * xr - gr * xi).astype(BF16)], axis=0
        )
        dks[:, cols] = jnp.dot(inv_lags[...], lag, preferred_element_type=F32).astype(BF16)

        for block in range(per_group):
            for row_block in range(row_blocks):
                owner = row_block * lane_blocks + i * per_group + block

                @pl.when(owner != me)
                def _():
                    rs_copy(owner, me).start()

        kr, ki = kspec[0:half, cols], kspec[half:, cols]
        y = jnp.concatenate(
            [(xr * kr - xi * ki).astype(BF16), (xr * ki + xi * kr).astype(BF16)], axis=0
        )
        z2[:, cols] = jnp.dot(inv_mixed[...], y, preferred_element_type=F32)
        return carry

    lax.fori_loop(0, groups, medium, 0)

    def backward(i, carry):
        cols = pl.ds(pl.multiple_of(i * group, group), group)

        @pl.when(has_after)
        def _():
            up_copy(i).wait_recv()

        d = gspec[:, cols] + jnp.dot(
            ahead[:, rows:length], up_in[:, cols], preferred_element_type=F32
        )
        dr, di = d[:half], d[half:]
        kr, ki = kspec[0:half, cols], kspec[half:, cols]
        y = jnp.concatenate(
            [(dr * kr + di * ki).astype(BF16), (di * kr - dr * ki).astype(BF16)], axis=0
        )
        dwide[...] = jnp.dot(inv_back[...], y, preferred_element_type=F32)

        for t, size in chunks(0, wide, 32):
            here = pl.ds(t, size)
            w = dwide[here, :] * alive[here, :]
            d2[0, here, :] = upstream[here, cols] * z2[here, cols]
            d2[1, here, :] = w * v2[here, cols]
            d2[2, here, :] = w * k2[here, cols]
        for part in range(3):
            d2[part, wide:, :] = d2[part, 1 : NEAR + 1, :]

        def mr_back(part, t, size):
            return sum(
                mrf[j, part : part + 1, cols] * d2[part, pl.ds(t + 8 * j, size), :]
                for j in range(feat)
            )

        for t, size in chunks(0, wide, 32):
            here = pl.ds(t, size)
            dy = mr_back(2, t, size)
            d1[0, here, :] = dy * z1[here, cols]
            dz1[here, :] = dy * q1[here, cols]
            outgoing[0, here, :] = mr_back(0, t, size).astype(BF16)
            outgoing[1, here, :] = mr_back(1, t, size).astype(BF16)
        dz1[wide:, :] = dz1[1 : FAR + 1, :]
        for part in range(2):
            out_mr[part, :, cols] = jnp.dot(
                unweave[...], outgoing[part], preferred_element_type=F32
            ).astype(BF16)

        sums = [jnp.zeros((8, group), F32) for _ in range(short)]
        for t, size in chunks(0, wide, 32):
            here = pl.ds(t, size)
            w = sum(sfilt[j : j + 1, cols] * dz1[pl.ds(t + 8 * j, size), :] for j in range(short))
            d1[1, here, :] = w * v1[here, cols]
            d1[2, here, :] = w * k1[here, cols]
            dz = dz1[here, :] * inner[here, :]
            for j in range(short):
                term = dz * pse[pl.ds(FAR + t - 8 * j, size), cols]
                for s in range(0, size, 8):
                    sums[j] = sums[j] + term[s : s + 8]
        for j in range(short):
            sks[j : j + 1, cols] = jnp.sum(sums[j], axis=0, keepdims=True)
        for part in range(3):
            d1[part, wide:, :] = d1[part, 1 : NEAR + 1, :]

        for part in range(3):
            for t, size in chunks(0, wide, 32):
                outgoing[2 + part, pl.ds(t, size), :] = sum(
                    sef[j, part : part + 1, cols] * d1[part, pl.ds(t + 8 * j, size), :]
                    for j in range(feat)
                ).astype(BF16)
            out_se[part, :, cols] = jnp.dot(
                unweave[...], outgoing[2 + part], preferred_element_type=F32
            ).astype(BF16)

        @pl.when(i == max(groups - 2, 0))
        def _():
            at_rows, at_cols = piece_of(me)
            rs[me] = dks[at_rows, at_cols]
            for_peers(lambda d: rs_copy(d, d).wait_recv())
            total = rs[0].astype(F32)
            for d in range(1, n_ctx):
                total = total + rs[d].astype(F32)
            ag[me] = total.astype(BF16)
            for_peers(lambda d: ag_copy(d, me).start())

        return carry

    lax.fori_loop(0, groups, backward, 0)

    _, my_cols = piece_of(me)
    for_peers(lambda d: srs_copy(d, me).start())
    srs[me] = sks[:, my_cols]
    scale = 1.0 / math.sqrt(rows * n_ctx)
    for_peers(lambda d: ag_copy(d, d).wait_recv())
    for d in range(n_ctx):
        r, c = (d // lane_blocks) * piece_rows, (d % lane_blocks) * lane_width
        out_medium[r : r + piece_rows, c : c + lane_width] = (
            ag[d].astype(F32) * damp[r : r + piece_rows, c : c + lane_width] * scale
        )
    for_peers(lambda d: srs_copy(d, d).wait_recv())
    total = srs[0]
    for d in range(1, n_ctx):
        total = total + srs[d]
    sag[me] = total * scale
    for_peers(lambda d: sag_copy(d, me).start())

    @pl.when(has_after)
    def _():
        for i in range(groups):
            for copy in to_after(i):
                copy.wait_send()
            hist_copy(i).wait_send()

    @pl.when(has_behind)
    def _():
        for i in range(groups):
            for copy in to_behind(i):
                copy.wait_send()
            up_copy(i).wait_send()

    for_peers(lambda d: rs_copy(d, me).wait_send())
    for_peers(lambda d: ag_copy(d, me).wait_send())
    for_peers(lambda d: srs_copy(d, me).wait_send())
    for_peers(lambda d: sag_copy(d, d).wait_recv())
    for d in range(lane_blocks):
        c = d * lane_width
        out_short[:, c : c + lane_width] = sag[d][0:short]
    for_peers(lambda d: sag_copy(d, me).wait_send())


def local(n_ctx, se_input, mr_input, cotangent, se_featurizer, mr_featurizer, se_filter, mr_filter, decay_rate):
    rows, channels = cotangent.shape
    taps, short, feat = mr_filter.shape[0], se_filter.shape[0], se_featurizer.shape[0]
    group = min(256, channels)
    groups = channels // group
    length, tables = transforms(rows, taps)
    lane_blocks = min(n_ctx, 8)
    lane_width = channels // lane_blocks
    piece_rows = taps // (n_ctx // lane_blocks)
    wide = rows + 2 * EDGE
    vmem = pltpu.VMEM
    dma = pltpu.SemaphoreType.DMA
    scratch = (
        [vmem((3, EDGE, channels), BF16), vmem((2, EDGE, channels), BF16)]
        + [vmem((3, EDGE, channels), BF16), vmem((EDGE, channels), BF16), vmem((EDGE, channels), BF16)]
        + [vmem((5, NEAR + wide, group), F32), vmem((NEAR + wide, group), F32)]
        + [vmem((wide, channels), F32)] * 3
        + [vmem((FAR + wide, channels), F32)]
        + [vmem((wide, channels), F32)] * 5
        + [vmem((taps, channels), BF16)] * 2
        + [vmem((length - rows, channels), BF16), vmem((taps + EDGE, channels), BF16)]
        + [vmem((wide, group), BF16)] * 2
        + [vmem((wide, group), F32)] * 2
        + [vmem((5, wide, group), BF16)]
        + [vmem((length, channels), F32)] * 3
        + [vmem((taps, channels), F32)]
        + [vmem((wide, group), F32), vmem((3, wide + NEAR, group), F32)]
        + [vmem((wide + FAR, group), F32), vmem((3, wide + NEAR, group), F32)]
        + [vmem((taps, channels), BF16)]
        + [vmem((n_ctx, piece_rows, lane_width), BF16)] * 2
        + [vmem((8, channels), F32)]
        + [vmem((n_ctx, 8, lane_width), F32)] * 2
        + [dma((5, groups))] * 2
        + [dma((groups,))] * 4
        + [dma((n_ctx,))] * 8
        + [vmem((3, rows, channels), BF16), vmem((2, rows, channels), BF16), vmem((rows, channels), BF16)]
        + [vmem(table.shape, BF16) for table in tables[2:]]
        + [dma((10,))]
    )
    out_se, out_mr, out_short, out_medium = pl.pallas_call(
        functools.partial(body, n_ctx, length, taps, short, feat, group),
        out_shape=(
            jax.ShapeDtypeStruct((3, rows, channels), BF16),
            jax.ShapeDtypeStruct((2, rows, channels), BF16),
            jax.ShapeDtypeStruct((short, channels), F32),
            jax.ShapeDtypeStruct((taps, channels), F32),
        ),
        in_specs=[pl.BlockSpec(memory_space=pl.ANY)] * 3
        + [pl.BlockSpec(memory_space=pltpu.VMEM)] * 7
        + [pl.BlockSpec(memory_space=pl.ANY)] * 7,
        out_specs=[pl.BlockSpec(memory_space=pltpu.VMEM)] * 4,
        scratch_shapes=scratch,
        compiler_params=pltpu.CompilerParams(
            collective_id=0, has_side_effects=True, vmem_limit_bytes=56 * 1024 * 1024
        ),
        cost_estimate=pl.CostEstimate(
            flops=12 * length * length * channels, bytes_accessed=14 * rows * channels * 2, transcendentals=0
        ),
        name="hyena_pair",
    )(
        jnp.transpose(se_input, (1, 0, 2)),
        jnp.transpose(mr_input, (1, 0, 2)),
        cotangent,
        se_featurizer,
        mr_featurizer,
        se_filter,
        mr_filter,
        decay_rate[None, :],
        *tables,
    )
    return jnp.transpose(out_se, (1, 0, 2)), jnp.transpose(out_mr, (1, 0, 2)), out_short, out_medium


def solution(mesh):
    placed = (
        P("ctx", None, "ts"),
        P("ctx", None, "ts"),
        P("ctx", "ts"),
        P(None, None, "ts"),
        P(None, None, "ts"),
        P(None, "ts"),
        P(None, "ts"),
        P("ts"),
    )
    return jax.shard_map(
        functools.partial(local, mesh.shape["ctx"]),
        mesh=mesh,
        in_specs=placed,
        out_specs=(P("ctx", None, "ts"), P("ctx", None, "ts"), P(None, "ts"), P(None, "ts")),
        check_vma=False,
    )
```
